32 devices in a mesh: parts: 2 (over x), lat: 16 (over z, y, core).
Axes of the slice: x: 2, y: 2, z: 4, core: 2. Of those that a mesh axis runs over, the one named last changes fastest.
Arguments:
- activations: bfloat16 [2, 1024, 1152], P(None, ('parts', 'lat')), parts along dimension 1, may hold values from -6 to 6
- enc_weight: bfloat16 [2, 1152, 65536], P(None, None, 'lat'), may hold values from -0.1875 to 0.1875
- enc_bias: float32 [2, 65536], P(None, 'lat'), may hold values from -1 to 0
- dec_weight: bfloat16 [3, 65536, 1152], P(None, 'lat'), may hold values from -0.0234375 to 0.0234375
- dec_bias: float32 [2, 1152], replicated, may hold values from -3 to 3
Outputs:
- reconstruction: float32 [1024, 2, 1152], P(('parts', 'lat')), parts along dimension 0
The draws below stay inside these ranges and needn't reach their ends.
There are 2 independent parts, one for each index of `parts`. The reference program is written for one: setup_inputs(seed, part) draws one part's arguments, and reference() takes and returns one part's arrays. A program takes and returns all parts, laid end to end along the dimension named above; an argument that names none is the same for every part. Nothing has to cross between parts.
All inputs are finite; a program needn't handle non-finite values.
Results may differ from the reference program's by a relative error of at most 0.0022.
Values may be sent and summed in bfloat16 or wider, within the bound.
A program may use at most 128 MiB of HBM per device.

```python
import jax
import jax.numpy as jnp

D = 1152
F = 65536
LAYERS = 2
PAIRS = 3
TOKENS = 512


def block_levels(rng, shape, shards, least, largest):
    loudness = 1.0
    for axis_at, blocks in shards:
        heights = jax.random.uniform(jax.random.fold_in(jax.random.fold_in(rng, 6), axis_at), (blocks,), jnp.float32, least / len(shards), largest / len(shards))
        loudness = loudness * jnp.repeat(jnp.exp(heights), shape[axis_at] // blocks).reshape((-1,) + (1,) * (len(shape) - 1 - axis_at))
    return loudness


def bell_draw(rng, dims, spread, most, pieces=(), held_as=jnp.bfloat16):
    factor_of = block_levels(rng, dims, pieces, -0.22, 0.18) if pieces else 1.0
    drawn = jax.random.normal(rng, dims, jnp.float32) * spread * factor_of
    return jnp.minimum(jnp.maximum(drawn, -most), most).astype(held_as)


def setup_inputs(seed: int = 0, part: int = 0) -> dict:
    splits = jax.random.split(jax.random.key(seed), 6)
    part_keys = jax.random.split(jax.random.fold_in(splits[5], part), 6)
    return {
        "activations": bell_draw(part_keys[0], (LAYERS, TOKENS, D), 1.0, 6.0, ((1, 16),)),
        "enc_weight": bell_draw(splits[1], (LAYERS, D, F), D ** -0.5, 0.1875, ((2, 16),)),
        "enc_bias": jnp.clip(-1.0 + 1.0 * jax.random.uniform(splits[2], (LAYERS, F), jnp.float32) ** block_levels(splits[2], (LAYERS, F), ((1, 16),), -0.2, 0.2), -1.0, 0.0),
        "dec_weight": bell_draw(splits[3], (PAIRS, F, D), F ** -0.5, 0.0234375, ((1, 16),)),
        "dec_bias": bell_draw(splits[4], (LAYERS, D), 0.5, 3.0, (), jnp.float32),
    }


def pair_index(source_layer, target_layer):
    return target_layer * (target_layer + 1) // 2 + source_layer


def reference(activations, enc_weight, enc_bias, dec_weight, dec_bias):
    latent_codes = []
    for source_layer in range(LAYERS):
        preact = jnp.dot(activations[source_layer], enc_weight[source_layer], preferred_element_type=jnp.float32)
        latent_codes.append(jax.nn.relu(preact + enc_bias[source_layer]).astype(jnp.bfloat16))
    targets_out = []
    for target_layer in range(LAYERS):
        partial_sum = jnp.zeros((TOKENS, D), jnp.float32)
        for source_layer in range(target_layer + 1):
            partial_sum = partial_sum + jnp.dot(latent_codes[source_layer], dec_weight[pair_index(source_layer, target_layer)], preferred_element_type=jnp.float32)
        targets_out.append(partial_sum + dec_bias[target_layer])
    return jnp.stack(targets_out, axis=1).astype(jnp.float32)
```

```python
import functools

import jax
import jax.numpy as jnp
from jax import lax
from jax.experimental import pallas as pl
from jax.experimental.pallas import tpu as pltpu
from jax.sharding import PartitionSpec as P

ENC_COLS = 512
OUT_COLS = 256
DEPTH = 2048


def pair_index(source_layer, target_layer):
    return target_layer * (target_layer + 1) // 2 + source_layer


def kernel(
    n, pieces,
    act, enc_w, enc_b, dec_w, dec_b,
    out,
    x, enc_buf, dec_buf, codes, part, core_in, y_out, y_in, z_out, z_in,
    own_sem, enc_sem, dec_sem,
    gz_s, gz_r, gy_s, gy_r, gc_s, gc_r,
    rc_s, rc_r, ry_s, ry_r, rz_s, rz_r,
):
    layers, rows, width = act.shape
    depth = n // 4
    chunks = enc_buf.shape[0]
    me = lax.axis_index("lat")
    c = lax.rem(me, 2)
    y = lax.rem(lax.div(me, 2), 2)
    z = lax.div(me, 4)

    def rank(zz, yy, cc):
        return zz * 4 + yy * 2 + cc

    def z_at(step):
        return lax.rem(z + step + depth, depth)

    y_peer = rank(z, 1 - y, c)
    c_peer = rank(z, y, 1 - c)
    z_peers = [rank(z_at(d), y, c) for d in range(depth)]
    z_froms = [rank(z_at(-d), y, c) for d in range(depth)]
    y_froms = [rank(z_at(-d), 1 - y, c) for d in range(depth)]

    def rows_of(l, r):
        return x.at[l, pl.ds(pl.multiple_of(r * rows, rows), rows)]

    def remote(src, dst, s, r, dev):
        return pltpu.make_async_remote_copy(
            src_ref=src, dst_ref=dst, send_sem=s, recv_sem=r,
            device_id={"lat": dev}, device_id_type=pl.DeviceIdType.MESH,
        )

    sent = []

    def start(copy):
        copy.start()
        sent.append(copy)

    def enc_copy(l, j):
        return pltpu.make_async_copy(
            enc_w.at[l, :, pl.ds(pl.multiple_of(j * ENC_COLS, ENC_COLS), ENC_COLS)],
            enc_buf.at[j], enc_sem.at[l, j],
        )

    def dec_copy(p):
        return pltpu.make_async_copy(dec_w.at[p], dec_buf.at[p], dec_sem.at[p])

    barrier = pltpu.get_barrier_semaphore()
    for dev in z_peers[1:] + [y_peer, c_peer]:
        pl.semaphore_signal(
            barrier, inc=1, device_id={"lat": dev}, device_id_type=pl.DeviceIdType.MESH
        )
    own = [pltpu.make_async_copy(act.at[l], rows_of(l, me), own_sem.at[l]) for l in range(layers)]
    for copy in own:
        copy.start()
    for j in range(chunks):
        enc_copy(0, j).start()
    pl.semaphore_wait(barrier, depth + 1)

    def gather_z(l):
        for d in range(1, depth):
            start(remote(act.at[l], rows_of(l, me), gz_s.at[l, d], gz_r.at[l, d], z_peers[d]))
        start(remote(act.at[l], rows_of(l, me), gy_s.at[l, 0], gy_r.at[l, 0], y_peer))
        start(remote(act.at[l], rows_of(l, me), gc_s.at[l, 0], gc_r.at[l, 0], c_peer))

    def gather_y(l):
        for d in range(1, depth):
            block = rows_of(l, z_froms[d])
            remote(block, block, gz_s.at[l, d], gz_r.at[l, d], me).wait_recv()
            start(remote(block, block, gy_s.at[l, d], gy_r.at[l, d], y_peer))
            start(remote(block, block, gc_s.at[l, d], gc_r.at[l, d], c_peer))

    def gather_core(l):
        for d in range(depth):
            block = rows_of(l, y_froms[d])
            remote(block, block, gy_s.at[l, d], gy_r.at[l, d], me).wait_recv()
            start(remote(block, block, gc_s.at[l, depth + d], gc_r.at[l, depth + d], c_peer))

    def gather_end(l):
        own[l].wait()
        for d in range(2 * depth):
            yy = y if d < depth else 1 - y
            block = rows_of(l, rank(z_at(-(d % depth)), yy, 1 - c))
            remote(block, block, gc_s.at[l, d], gc_r.at[l, d], me).wait_recv()

    def encode(l, first, last):
        def body(j, carry):
            enc_copy(l, j).wait()
            cols = pl.ds(pl.multiple_of(j * ENC_COLS, ENC_COLS), ENC_COLS)
            pre = jnp.dot(x[l], enc_buf[j], preferred_element_type=jnp.float32)
            code = jnp.maximum(pre + enc_b[l : l + 1, cols], 0.0)
            codes[l, :, cols] = code.astype(jnp.bfloat16)
            if l + 1 < layers:
                enc_copy(l + 1, j).start()
            return carry

        lax.fori_loop(first, last, body, 0)

    def decode(q, s):
        t, at, wide = pieces[q]
        p = pair_index(s, t)
        step = min(DEPTH, codes.shape[2])
        total = None
        for k in range(0, codes.shape[2], step):
            term = jnp.dot(
                codes[s, :, k : k + step],
                dec_buf[p, k : k + step, at : at + wide],
                preferred_element_type=jnp.float32,
            )
            total = term if total is None else total + term
        total = total.reshape(depth, 2, 2, rows, wide)
        if s > 0:
            total = total + part[q, :, :, :, :, :wide]
        part[q, :, :, :, :, :wide] = total

    def to_core(q):
        wide = pieces[q][2]
        return remote(
            part.at[q, :, :, 1 - c, :, pl.ds(0, wide)], core_in.at[q, :, :, :, pl.ds(0, wide)],
            rc_s.at[q], rc_r.at[q], c_peer,
        )

    def to_y(q):
        cols = pl.ds(0, pieces[q][2])
        return remote(
            y_out.at[q, :, :, cols], y_in.at[q, :, :, cols], ry_s.at[q], ry_r.at[q], y_peer
        )

    def to_z(q, d):
        cols = pl.ds(0, pieces[q][2])
        return remote(
            z_out.at[q, z_at(d), :, cols], z_in.at[q, d, :, cols],
            rz_s.at[q, d], rz_r.at[q, d], z_peers[d],
        )

    def stage_core(q):
        start(to_core(q))

    def stage_y(q):
        wide = pieces[q][2]
        to_core(q).wait_recv()
        away = part[q, :, 1 - y, c, :, :wide] + core_in[q, :, 1 - y, :, :wide]
        y_out[q, :, :, :wide] = away.astype(jnp.bfloat16)
        start(to_y(q))
        part[q, :, y, c, :, :wide] = part[q, :, y, c, :, :wide] + core_in[q, :, y, :, :wide]

    def stage_z(q):
        wide = pieces[q][2]
        to_y(q).wait_recv()
        total = part[q, :, y, c, :, :wide] + y_in[q, :, :, :wide].astype(jnp.float32)
        z_out[q, :, :, :wide] = total.astype(jnp.bfloat16)
        for d in range(1, depth):
            start(to_z(q, d))
        part[q, :, y, c, :, :wide] = total

    def stage_out(q):
        t, at, wide = pieces[q]
        total = part[q, z, y, c, :, :wide] + dec_b[t : t + 1, at : at + wide]
        for d in range(1, depth):
            to_z(q, d).wait_recv()
            total = total + z_in[q, d, :, :wide].astype(jnp.float32)
        out[t, :, at : at + wide] = total

    stages = (stage_core, stage_y, stage_z, stage_out)
    offsets = (0, 1, 3, 5)
    due = []
    clock = [0]

    def tick():
        now = [e for e in due if e[0] <= clock[0]]
        for e in sorted(now):
            due.remove(e)
            stages[e[2]](e[1])
        clock[0] += 1

    def finished(q):
        for k, o in enumerate(offsets):
            due.append((clock[0] + o, q, k))

    gather_z(0)
    gather_y(0)
    gather_core(0)
    dec_copy(0).start()
    for l in range(1, layers):
        gather_z(l)
    gather_end(0)

    half = chunks // 2
    for t in range(layers):
        if t == 0:
            encode(0, 0, half)
            for l in range(1, layers):
                gather_y(l)
            encode(0, half, chunks)
            for p in range(1, dec_buf.shape[0]):
                dec_copy(p).start()
        else:
            if t == 1:
                for l in range(1, layers):
                    gather_core(l)
            gather_end(t)
            for a in range(0, chunks, 2):
                encode(t, a, a + 2)
                tick()
        for s in range(t + 1):
            dec_copy(pair_index(s, t)).wait()
        for q in range(len(pieces)):
            if pieces[q][0] != t:
                continue
            for s in range(t + 1):
                decode(q, s)
                if s == t:
                    finished(q)
                tick()
    while due:
        tick()
    for copy in sent:
        copy.wait_send()


def on_device(activations, enc_weight, enc_bias, dec_weight, dec_bias):
    layers, rows, width = activations.shape
    latents = enc_weight.shape[2]
    pairs = dec_weight.shape[0]
    n = lax.axis_size("lat")
    depth = n // 4
    tokens = n * rows
    chunks = latents // ENC_COLS
    pieces = [
        (t, at, min(OUT_COLS, width - at)) for t in range(layers) for at in range(0, width, OUT_COLS)
    ]
    count = len(pieces)
    vmem = pl.BlockSpec(memory_space=pltpu.VMEM)
    hbm = pl.BlockSpec(memory_space=pl.ANY)
    dma = pltpu.SemaphoreType.DMA
    bf16, f32 = jnp.bfloat16, jnp.float32
    result = pl.pallas_call(
        functools.partial(kernel, n, pieces),
        out_shape=jax.ShapeDtypeStruct((layers, rows, width), f32),
        in_specs=[hbm, hbm, vmem, hbm, vmem],
        out_specs=vmem,
        scratch_shapes=[
            pltpu.VMEM((layers, tokens, width), bf16),
            pltpu.VMEM((chunks, width, ENC_COLS), bf16),
            pltpu.VMEM((pairs, latents, width), bf16),
            pltpu.VMEM((layers, tokens, latents), bf16),
            pltpu.VMEM((count, depth, 2, 2, rows, OUT_COLS), f32),
            pltpu.VMEM((count, depth, 2, rows, OUT_COLS), f32),
            pltpu.VMEM((count, depth, rows, OUT_COLS), bf16),
            pltpu.VMEM((count, depth, rows, OUT_COLS), bf16),
            pltpu.VMEM((count, depth, rows, OUT_COLS), bf16),
            pltpu.VMEM((count, depth, rows, OUT_COLS), bf16),
            dma((layers,)),
            dma((layers, chunks)),
            dma((pairs,)),
            dma((layers, depth)), dma((layers, depth)),
            dma((layers, depth)), dma((layers, depth)),
            dma((layers, 2 * depth)), dma((layers, 2 * depth)),
            dma((count,)), dma((count,)),
            dma((count,)), dma((count,)),
            dma((count, depth)), dma((count, depth)),
        ],
        compiler_params=pltpu.CompilerParams(
            collective_id=0, has_side_effects=True, vmem_limit_bytes=63 * 1024 * 1024
        ),
        cost_estimate=pl.CostEstimate(
            flops=2 * tokens * latents * width * (layers + pairs),
            bytes_accessed=2 * latents * width * (layers + pairs),
            transcendentals=0,
        ),
    )(activations, enc_weight, enc_bias, dec_weight, dec_bias)
    return jnp.transpose(result, (1, 0, 2))


def solution(mesh):
    placed = (
        P(None, ("parts", "lat"), None),
        P(None, None, "lat"),
        P(None, "lat"),
        P(None, "lat", None),
        P(),
    )
    return jax.shard_map(
        on_device,
        mesh=mesh,
        in_specs=placed,
        out_specs=P(("parts", "lat"), None, None),
        check_vma=False,
    )
```

```python
import functools

import jax
import jax.numpy as jnp
from jax import lax
from jax.experimental import pallas as pl
from jax.experimental.pallas import tpu as pltpu
from jax.sharding import PartitionSpec as P

ENC_COLS = 512
OUT_COLS = 256
DEPTH = 2048


def pair_index(source_layer, target_layer):
    return target_layer * (target_layer + 1) // 2 + source_layer


def kernel(
    n, pieces,
    act, enc_w, enc_b, dec_w, dec_b,
    out,
    x, enc_buf, dec_buf, codes, part, core_in, y_out, y_in, z_out, z_in,
    own_sem, enc_sem, dec_sem,
    gz_s, gz_r, gy_s, gy_r, gc_s, gc_r,
    rc_s, rc_r, ry_s, ry_r, rz_s, rz_r,
):
    layers, rows, width = act.shape
    depth = n // 4
    chunks = enc_buf.shape[0]
    me = lax.axis_index("lat")
    c = lax.rem(me, 2)
    y = lax.rem(lax.div(me, 2), 2)
    z = lax.div(me, 4)

    def rank(zz, yy, cc):
        return zz * 4 + yy * 2 + cc

    def z_at(step):
        return lax.rem(z + step + depth, depth)

    y_peer = rank(z, 1 - y, c)
    c_peer = rank(z, y, 1 - c)
    z_peers = [rank(z_at(d), y, c) for d in range(depth)]
    z_froms = [rank(z_at(-d), y, c) for d in range(depth)]
    y_froms = [rank(z_at(-d), 1 - y, c) for d in range(depth)]

    def rows_of(l, r):
        return x.at[l, pl.ds(pl.multiple_of(r * rows, rows), rows)]

    def remote(src, dst, s, r, dev):
        return pltpu.make_async_remote_copy(
            src_ref=src, dst_ref=dst, send_sem=s, recv_sem=r,
            device_id={"lat": dev}, device_id_type=pl.DeviceIdType.MESH,
        )

    sent = []

    def start(copy):
        copy.start()
        sent.append(copy)

    def enc_copy(l, j):
        return pltpu.make_async_copy(
            enc_w.at[l, :, pl.ds(pl.multiple_of(j * ENC_COLS, ENC_COLS), ENC_COLS)],
            enc_buf.at[j], enc_sem.at[l, j],
        )

    def dec_copy(p):
        return pltpu.make_async_copy(dec_w.at[p], dec_buf.at[p], dec_sem.at[p])

    barrier = pltpu.get_barrier_semaphore()
    for dev in z_peers[1:] + [y_peer, c_peer]:
        pl.semaphore_signal(
            barrier, inc=1, device_id={"lat": dev}, device_id_type=pl.DeviceIdType.MESH
        )
    own = [pltpu.make_async_copy(act.at[l], rows_of(l, me), own_sem.at[l]) for l in range(layers)]
    for copy in own:
        copy.start()
    for j in range(chunks):
        enc_copy(0, j).start()
    pl.semaphore_wait(barrier, depth + 1)

    def gather_z(l):
        for d in range(1, depth):
            start(remote(act.at[l], rows_of(l, me), gz_s.at[l, d], gz_r.at[l, d], z_peers[d]))
        start(remote(act.at[l], rows_of(l, me), gy_s.at[l, 0], gy_r.at[l, 0], y_peer))
        start(remote(act.at[l], rows_of(l, me), gc_s.at[l, 0], gc_r.at[l, 0], c_peer))

    def gather_y(l):
        for d in range(1, depth):
            block = rows_of(l, z_froms[d])
            remote(block, block, gz_s.at[l, d], gz_r.at[l, d], me).wait_recv()
            start(remote(block, block, gy_s.at[l, d], gy_r.at[l, d], y_peer))
            start(remote(block, block, gc_s.at[l, d], gc_r.at[l, d], c_peer))

    def gather_core(l):
        for d in range(depth):
            block = rows_of(l, y_froms[d])
            remote(block, block, gy_s.at[l, d], gy_r.at[l, d], me).wait_recv()
            start(remote(block, block, gc_s.at[l, depth + d], gc_r.at[l, depth + d], c_peer))

    def gather_end(l):
        own[l].wait()
        for d in range(2 * depth):
            yy = y if d < depth else 1 - y
            block = rows_of(l, rank(z_at(-(d % depth)), yy, 1 - c))
            remote(block, block, gc_s.at[l, d], gc_r.at[l, d], me).wait_recv()

    def encode(l, first, last):
        def body(j, carry):
            enc_copy(l, j).wait()
            cols = pl.ds(pl.multiple_of(j * ENC_COLS, ENC_COLS), ENC_COLS)
            pre = jnp.dot(x[l], enc_buf[j], preferred_element_type=jnp.float32)
            code = jnp.maximum(pre + enc_b[l : l + 1, cols], 0.0)
            codes[l, :, cols] = code.astype(jnp.bfloat16)
            if l + 1 < layers:
                enc_copy(l + 1, j).start()
            return carry

        lax.fori_loop(first, last, body, 0)

    def decode(q, s):
        t, at, wide = pieces[q]
        p = pair_index(s, t)
        step = min(DEPTH, codes.shape[2])
        total = None
        for k in range(0, codes.shape[2], step):
            term = jnp.dot(
                codes[s, :, k : k + step],
                dec_buf[p, k : k + step, at : at + wide],
                preferred_element_type=jnp.float32,
            )
            total = term if total is None else total + term
        total = total.reshape(depth, 2, 2, rows, wide)
        if s > 0:
            total = total + part[q, :, :, :, :, :wide]
        part[q, :, :, :, :, :wide] = total

    def to_core(q):
        wide = pieces[q][2]
        return remote(
            part.at[q, :, :, 1 - c, :, pl.ds(0, wide)], core_in.at[q, :, :, :, pl.ds(0, wide)],
            rc_s.at[q], rc_r.at[q], c_peer,
        )

    def to_y(q):
        cols = pl.ds(0, pieces[q][2])
        return remote(
            y_out.at[q, :, :, cols], y_in.at[q, :, :, cols], ry_s.at[q], ry_r.at[q], y_peer
        )

    def to_z(q, d):
        cols = pl.ds(0, pieces[q][2])
        return remote(
            z_out.at[q, z_at(d), :, cols], z_in.at[q, d, :, cols],
            rz_s.at[q, d], rz_r.at[q, d], z_peers[d],
        )

    def stage_core(q):
        start(to_core(q))

    def stage_y(q):
        wide = pieces[q][2]
        to_core(q).wait_recv()
        away = part[q, :, 1 - y, c, :, :wide] + core_in[q, :, 1 - y, :, :wide]
        y_out[q, :, :, :wide] = away.astype(jnp.bfloat16)
        start(to_y(q))
        part[q, :, y, c, :, :wide] = part[q, :, y, c, :, :wide] + core_in[q, :, y, :, :wide]

    def stage_z(q):
        wide = pieces[q][2]
        to_y(q).wait_recv()
        total = part[q, :, y, c, :, :wide] + y_in[q, :, :, :wide].astype(jnp.float32)
        z_out[q, :, :, :wide] = total.astype(jnp.bfloat16)
        for d in range(1, depth):
            start(to_z(q, d))
        part[q, :, y, c, :, :wide] = total

    def stage_out(q):
        t, at, wide = pieces[q]
        total = part[q, z, y, c, :, :wide] + dec_b[t : t + 1, at : at + wide]
        for d in range(1, depth):
            to_z(q, d).wait_recv()
            total = total + z_in[q, d, :, :wide].astype(jnp.float32)
        out[t, :, at : at + wide] = total

    stages = (stage_core, stage_y, stage_z, stage_out)
    offsets = (0, 2, 6, 10)
    due = []
    clock = [0]

    def tick():
        now = [e for e in due if e[0] <= clock[0]]
        for e in sorted(now):
            due.remove(e)
            stages[e[2]](e[1])
        clock[0] += 1

    def finished(q):
        for k, o in enumerate(offsets):
            due.append((clock[0] + o, q, k))

    gather_z(0)
    gather_y(0)
    gather_core(0)
    dec_copy(0).start()
    for l in range(1, layers):
        gather_z(l)
    gather_end(0)

    half = chunks // 2
    for t in range(layers):
        if t == 0:
            encode(0, 0, half)
            for l in range(1, layers):
                gather_y(l)
            encode(0, half, chunks)
            for p in range(1, dec_buf.shape[0]):
                dec_copy(p).start()
        else:
            if t == 1:
                for l in range(1, layers):
                    gather_core(l)
            gather_end(t)
            for a in range(0, chunks, 2):
                encode(t, a, a + 2)
                tick()
        for s in range(t + 1):
            dec_copy(pair_index(s, t)).wait()
        for q in range(len(pieces)):
            if pieces[q][0] != t:
                continue
            for s in range(t + 1):
                decode(q, s)
                if s == t:
                    finished(q)
                tick()
    while due:
        tick()
    for copy in sent:
        copy.wait_send()


def on_device(activations, enc_weight, enc_bias, dec_weight, dec_bias):
    layers, rows, width = activations.shape
    latents = enc_weight.shape[2]
    pairs = dec_weight.shape[0]
    n = lax.axis_size("lat")
    depth = n // 4
    tokens = n * rows
    chunks = latents // ENC_COLS
    pieces = [
        (t, at, min(OUT_COLS, width - at)) for t in range(layers) for at in range(0, width, OUT_COLS)
    ]
    count = len(pieces)
    vmem = pl.BlockSpec(memory_space=pltpu.VMEM)
    hbm = pl.BlockSpec(memory_space=pl.ANY)
    dma = pltpu.SemaphoreType.DMA
    bf16, f32 = jnp.bfloat16, jnp.float32
    result = pl.pallas_call(
        functools.partial(kernel, n, pieces),
        out_shape=jax.ShapeDtypeStruct((layers, rows, width), f32),
        in_specs=[hbm, hbm, vmem, hbm, vmem],
        out_specs=vmem,
        scratch_shapes=[
            pltpu.VMEM((layers, tokens, width), bf16),
            pltpu.VMEM((chunks, width, ENC_COLS), bf16),
            pltpu.VMEM((pairs, latents, width), bf16),
            pltpu.VMEM((layers, tokens, latents), bf16),
            pltpu.VMEM((count, depth, 2, 2, rows, OUT_COLS), f32),
            pltpu.VMEM((count, depth, 2, rows, OUT_COLS), f32),
            pltpu.VMEM((count, depth, rows, OUT_COLS), bf16),
            pltpu.VMEM((count, depth, rows, OUT_COLS), bf16),
            pltpu.VMEM((count, depth, rows, OUT_COLS), bf16),
            pltpu.VMEM((count, depth, rows, OUT_COLS), bf16),
            dma((layers,)),
            dma((layers, chunks)),
            dma((pairs,)),
            dma((layers, depth)), dma((layers, depth)),
            dma((layers, depth)), dma((layers, depth)),
            dma((layers, 2 * depth)), dma((layers, 2 * depth)),
            dma((count,)), dma((count,)),
            dma((count,)), dma((count,)),
            dma((count, depth)), dma((count, depth)),
        ],
        compiler_params=pltpu.CompilerParams(
            collective_id=0, has_side_effects=True, vmem_limit_bytes=63 * 1024 * 1024
        ),
        cost_estimate=pl.CostEstimate(
            flops=2 * tokens * latents * width * (layers + pairs),
            bytes_accessed=2 * latents * width * (layers + pairs),
            transcendentals=0,
        ),
    )(activations, enc_weight, enc_bias, dec_weight, dec_bias)
    return jnp.transpose(result, (1, 0, 2))


def solution(mesh):
    placed = (
        P(None, ("parts", "lat"), None),
        P(None, None, "lat"),
        P(None, "lat"),
        P(None, "lat", None),
        P(),
    )
    return jax.shard_map(
        on_device,
        mesh=mesh,
        in_specs=placed,
        out_specs=P(("parts", "lat"), None, None),
        check_vma=False,
    )
```
